512 devices in a mesh: fx: 8 (over z_lo, core), fy: 16 (over y, x), dp: 4 (over z_hi).
Axes of the slice: x: 4, y: 4, z: 16 (z_hi: 4, z_lo: 4; z = z_hi * 4 + z_lo), core: 2. Of those that a mesh axis runs over, the one named last changes fastest.
Arguments:
- hidden_in: bfloat16 [4, 128, 128, 1152], P('dp', ('fx', 'fy')), may hold values from -6 to 6
- spatial_triple: bfloat16 [4, 128, 128, 1728], P('dp', ('fx', 'fy')), may hold values from -6 to 6
- context_grad: bfloat16 [4, 128, 128, 576], P('dp', None, ('fx', 'fy')), may hold values from -6 to 6
- out_weight: bfloat16 [576, 1152], P(None, ('fx', 'fy')), may hold values from -0.25 to 0.25
- triple_weight: bfloat16 [1152, 1728], P(('fx', 'fy')), may hold values from -0.1875 to 0.1875
Outputs:
- grad_triple: bfloat16 [4, 128, 128, 1728], P('dp', ('fx', 'fy'))
- grad_hidden: bfloat16 [4, 128, 128, 1152], P('dp', ('fx', 'fy'))
- grad_out_weight: float32 [576, 1152], P(None, ('fx', 'fy'))
The draws below stay inside these ranges and needn't reach their ends.
All inputs are finite; a program needn't handle non-finite values.
Results may differ from the reference program's by a relative error of at most 0.03.
Values may be sent and summed in bfloat16 or wider, within the bound.
No kernel may reach another device: no remote copies, remote signals or barrier semaphores. Data moves between devices by JAX's collectives and lax.ppermute only.
A program may use at most 64 MiB of HBM per device.

```python
import math
from functools import partial
import jax
import jax.numpy as jnp
from jax import lax

D = 1152
HEADS = 8
INNER = 576
FRAMES = 128
PATCHES = 128
CLIPS = 4


def level_of(stream_key, extent, split, least, largest):
    level = 1.0
    for axis_at, blocks in split:
        draws = jax.random.uniform(jax.random.fold_in(jax.random.fold_in(stream_key, 6), axis_at), (blocks,), jnp.float32, least / len(split), largest / len(split))
        level = level * jnp.repeat(jnp.exp(draws), extent[axis_at] // blocks).reshape((-1,) + (1,) * (len(extent) - 1 - axis_at))
    return level


def scatter_about(rng, dims, scale, reach, pieces=(), kind=jnp.bfloat16):
    level = level_of(rng, dims, pieces, -0.22, 0.18) if pieces else 1.0
    values = jax.random.normal(rng, dims, jnp.float32) * scale * level
    return jnp.minimum(jnp.maximum(values, -reach), reach).astype(kind)


def setup_inputs(seed: int = 0) -> dict:
    seeds = jax.random.split(jax.random.key(seed), 6)
    return {
        "hidden_in": scatter_about(seeds[0], (CLIPS, FRAMES, PATCHES, D), 1.0, 6.0, ((0, 4), (1, 128))),
        "spatial_triple": scatter_about(seeds[1], (CLIPS, FRAMES, PATCHES, 3 * INNER), 1.0, 6.0, ((0, 4), (1, 128))),
        "context_grad": scatter_about(seeds[2], (CLIPS, FRAMES, PATCHES, INNER), 1.0, 6.0, ((0, 4), (2, 128))),
        "out_weight": scatter_about(seeds[3], (INNER, D), INNER ** -0.5, 0.25, ((1, 128),)),
        "triple_weight": scatter_about(seeds[4], (D, 3 * INNER), D ** -0.5, 0.1875, ((0, 128),)),
    }


def attention(triple, heads):
    batch, length, total_width = triple.shape
    size_head = total_width // (3 * heads)
    parts = triple.reshape(batch, length, 3, heads, size_head)
    query = parts[:, :, 0]
    keys = parts[:, :, 1]
    values = parts[:, :, 2]
    scores = jnp.einsum('bqhe,bkhe->bhqk', query, keys, precision=lax.Precision.HIGHEST) / math.sqrt(size_head)
    weights = jnp.exp(scores)
    weights = weights / lax.optimization_barrier(jnp.sum(weights, axis=-1, keepdims=True))
    output = jnp.einsum('bhqk,bkhe->bqhe', weights, values, precision=lax.Precision.HIGHEST)
    return output.reshape(batch, length, heads * size_head)

def normalize(hidden):
    centre = lax.optimization_barrier(jnp.mean(hidden, axis=-1, keepdims=True))
    centred = hidden - centre
    spread = lax.optimization_barrier(jnp.mean(centred * centred, axis=-1, keepdims=True))
    return centred * lax.rsqrt(spread + 1e-06)

def reference(hidden_in, spatial_triple, context_grad, out_weight, triple_weight):

    def one_clip(carry, inputs):
        tokens, triple, cotangent = inputs
        frames, patches, width = tokens.shape
        count = frames * patches
        spatial_in = triple.astype(jnp.float32)
        context_f32, spatial_back = jax.vjp(partial(attention, heads=HEADS), spatial_in)
        context = context_f32.astype(jnp.bfloat16).reshape(count, -1)
        mixed = jnp.dot(context, out_weight, preferred_element_type=jnp.float32)
        hidden = (tokens.reshape(count, width).astype(jnp.float32) + mixed).astype(jnp.bfloat16)
        normed = normalize(hidden.astype(jnp.float32)).astype(jnp.bfloat16)
        temporal = jnp.dot(normed, triple_weight, preferred_element_type=jnp.float32).astype(jnp.bfloat16)
        columns = jnp.transpose(temporal.reshape(frames, patches, -1), (1, 0, 2)).astype(jnp.float32)
        unused, temporal_back = jax.vjp(partial(attention, heads=HEADS), columns)
        column_cot = jnp.transpose(cotangent, (1, 0, 2)).astype(jnp.float32)
        grad_columns = temporal_back(column_cot)[0].astype(jnp.bfloat16)
        grad_temporal = jnp.transpose(grad_columns, (1, 0, 2)).reshape(count, -1)
        grad_normed = jnp.dot(grad_temporal, triple_weight.T, preferred_element_type=jnp.float32)
        unused_norm, norm_back = jax.vjp(normalize, hidden.astype(jnp.float32))
        grad_hidden = norm_back(grad_normed)[0].astype(jnp.bfloat16)
        weight_term = jnp.dot(context.T, grad_hidden, preferred_element_type=jnp.float32)
        grad_context = jnp.dot(grad_hidden, out_weight.T, preferred_element_type=jnp.float32)
        grad_triple = spatial_back(grad_context.reshape(frames, patches, -1))[0].astype(jnp.bfloat16)
        return (carry + weight_term, (grad_triple, grad_hidden.reshape(frames, patches, width)))
    start = jnp.zeros((INNER, D), jnp.float32)
    total, outputs = lax.scan(one_clip, start, (hidden_in, spatial_triple, context_grad))
    return (outputs[0], outputs[1], total / CLIPS)
```

```python
import math

import numpy as np
import jax
import jax.numpy as jnp
from jax import lax
from jax.experimental import pallas as pl
from jax.experimental.pallas import tpu as pltpu
from jax.sharding import PartitionSpec as P

HEADS = 8
SIZE = 72
INNER = HEADS * SIZE
D = 1152
TOKENS = 128
GX, GY = 8, 16
ROWS = 9
BF = jnp.bfloat16
F32 = jnp.float32
SCALE = 1.0 / math.sqrt(SIZE)
PARAMS = pltpu.CompilerParams(vmem_limit_bytes=48 * 1024 * 1024)

_place = np.arange(D)
_j, _i, _r = _place // 72, (_place // 9) % 8, _place % 9
FEATURE_AT = ((_i * GY + _j) * ROWS + _r).astype(np.int32)
PLACE_OF = np.argsort(FEATURE_AT).astype(np.int32)
_t = np.arange(TOKENS)
ROW_AT = ((_t % 8) * 16 + _t // 8).astype(np.int32)
ROW_BACK = ((_t % 16) * 8 + _t // 16).astype(np.int32)
_c = np.arange(640)
HALF_A = np.where(_c % 40 < 36, (_c // 40) * 72 + _c % 40, -1).astype(np.int32)
HALF_B = np.where(_c % 40 < 36, (_c // 40) * 72 + 36 + _c % 40, -1).astype(np.int32)
_s = np.arange(32)
FIRST_ROWS = ((_s // 8) * 9 + _s % 8).astype(np.int32)
LAST_ROW = np.where(_s % 8 == 0, (_s // 8) * 9 + 8, -1).astype(np.int32)


def dot(a, b, dims):
    return lax.dot_general(a, b, (dims, ((), ())), preferred_element_type=F32)


def nn(a, b):
    return dot(a, b, ((1,), (0,)))


def nt(a, b):
    return dot(a, b, ((1,), (1,)))


def tn(a, b):
    return dot(a, b, ((0,), (0,)))


def pick_columns(rows, source):
    at = lax.broadcasted_iota(jnp.int32, (rows, source.shape[1]), 0)
    return jnp.where(at == source, 1.0, 0.0).astype(BF)


def pick_rows(source, columns):
    at = lax.broadcasted_iota(jnp.int32, (source.shape[0], columns), 1)
    return jnp.where(at == source, 1.0, 0.0).astype(BF)


def stack_heads(x):
    lane = lax.broadcasted_iota(jnp.int32, (1, INNER), 1)
    parts = []
    for h in range(HEADS):
        mask = jnp.where((lane >= h * SIZE) & (lane < (h + 1) * SIZE), 1.0, 0.0).astype(BF)
        parts.append(x * mask)
    return jnp.concatenate(parts, axis=0)


def head_of(x, h):
    return x[:, h * TOKENS:(h + 1) * TOKENS]


def softmax(scores):
    shifted = scores * SCALE
    top = jnp.max(shifted, axis=-1, keepdims=True)
    e = jnp.exp(shifted - top)
    return e / jnp.sum(e, axis=-1, keepdims=True)


def attend(q, k, v):
    scores = nt(q, stack_heads(k))
    weights = [softmax(head_of(scores, h)).astype(BF) for h in range(HEADS)]
    return nn(jnp.concatenate(weights, axis=1), stack_heads(v))


def attend_back(q, k, v, cot):
    stacked_k = stack_heads(k)
    scores = nt(q, stacked_k)
    grad_weights = nt(cot, stack_heads(v))
    weights, grad_scores = [], []
    for h in range(HEADS):
        p = softmax(head_of(scores, h))
        g = head_of(grad_weights, h)
        mean = jnp.sum(p * g, axis=-1, keepdims=True)
        weights.append(p.astype(BF))
        grad_scores.append((p * (g - mean) * SCALE).astype(BF))
    grad_q = nn(jnp.concatenate(grad_scores, axis=1), stacked_k)
    grad_k = tn(jnp.concatenate(grad_scores, axis=0), stack_heads(q))
    grad_v = tn(jnp.concatenate(weights, axis=0), stack_heads(cot))
    return grad_q, grad_k, grad_v


def split_triple(triple):
    return triple[:, :INNER], triple[:, INNER:2 * INNER], triple[:, 2 * INNER:]


def gather_kernel(packed, out_copies, triple_rows, held):
    for i in range(GX):
        held[i * ROWS:(i + 1) * ROWS, :] = packed[i].astype(F32)
    rows = held[...]
    part = rows[:, :INNER].astype(BF)
    for j in range(GY):
        out_copies[j] = part
    triple_rows[...] = rows[:, INNER:].astype(BF)


def context_kernel(triple, hidden_in, feature_at, context, hidden_placed):
    q, k, v = split_triple(triple[...])
    context[...] = attend(q, k, v).astype(BF)
    hidden_placed[...] = nn(hidden_in[...], pick_columns(D, feature_at[...])).astype(BF)


def hidden_kernel(context, hidden_placed, out_rows, row_at, payload):
    ctx = context[...]
    hidden = (hidden_placed[...].astype(F32) + nt(ctx, out_rows[...])).astype(BF)
    turn = pick_rows(row_at[...], TOKENS)
    payload[:, :D] = nn(turn, hidden).astype(BF)
    payload[:, D:] = nn(turn, ctx).astype(BF)


def temporal_kernel(payload, weight, cotangent, row_at, half_a, half_b, message):
    hidden = payload[:, :D].astype(F32)
    ctx = payload[:, D:]
    centred = hidden - jnp.mean(hidden, axis=-1, keepdims=True)
    scale = lax.rsqrt(jnp.mean(centred * centred, axis=-1, keepdims=True) + 1e-06)
    normal = centred * scale
    w = weight[...]
    triple = nn(normal.astype(BF), w).astype(BF)
    q, k, v = split_triple(triple)
    grads = attend_back(q, k, v, cotangent[...])
    grad_triple = jnp.concatenate(grads, axis=1).astype(BF)
    grad_normal = nt(grad_triple, w)
    along = jnp.mean(grad_normal * normal, axis=-1, keepdims=True)
    level = jnp.mean(grad_normal, axis=-1, keepdims=True)
    grad_hidden = (scale * (grad_normal - level - normal * along)).astype(BF)
    turned = nn(pick_rows(row_at[...], TOKENS), grad_hidden)
    halves = jnp.concatenate(
        [
            nn(grad_hidden, pick_columns(D, half_a[...])).astype(BF),
            nn(grad_hidden, pick_columns(D, half_b[...])).astype(BF),
        ],
        axis=0,
    )
    ctx32 = ctx.astype(F32)
    blank = jnp.zeros((TOKENS, INNER), F32)
    sides = jnp.concatenate(
        [
            jnp.concatenate([ctx32, blank], axis=1),
            jnp.concatenate([blank, ctx32], axis=1),
        ],
        axis=0,
    ).astype(BF)
    term = tn(halves, sides)
    for j in range(GY):
        message[j] = jnp.concatenate(
            [term[j * 40:(j + 1) * 40], turned[j * 8:(j + 1) * 8]], axis=0
        ).astype(BF)


def turn_kernel(received, row_back, first_rows, last_row, message):
    total = received[0].astype(F32)
    parts = [total[40:]]
    total = total[:40]
    for j in range(1, GY):
        one = received[j].astype(F32)
        parts.append(one[40:])
        total = total + one[:40]
    grad = jnp.concatenate(parts, axis=0).astype(BF)
    turned = nn(pick_rows(row_back[...], TOKENS), grad)
    first = pick_rows(first_rows[...], 40)
    last = pick_rows(last_row[...], 40)
    for half in range(2):
        part = total[:, half * INNER:(half + 1) * INNER].astype(BF)
        both = jnp.concatenate([nn(first, part), nn(last, part)], axis=1)
        for low in range(4):
            i = half * 4 + low
            message[i] = jnp.concatenate(
                [turned[i * 16:(i + 1) * 16], both[low * 8:(low + 1) * 8]], axis=0
            ).astype(BF)


def sum_kernel(received, total):
    s = received[0, 16:, :].astype(F32)
    for i in range(1, GX):
        s = s + received[i, 16:, :].astype(F32)
    total[:8] = s[:, :INNER]
    total[8:] = s[:, INNER:]


def final_kernel(received, out_rows, triple, place_of, grad_triple, grad_hidden):
    grad = jnp.concatenate([received[i, :16, :] for i in range(GX)], axis=0)
    grad_hidden[...] = nn(grad, pick_columns(D, place_of[...])).astype(BF)
    cot = nn(grad, out_rows[...]).astype(BF)
    q, k, v = split_triple(triple[...])
    grad_triple[...] = jnp.concatenate(attend_back(q, k, v, cot), axis=1).astype(BF)


def call(kernel, name, outs, *args, scratch=()):
    many = isinstance(outs, list)
    shapes = [jax.ShapeDtypeStruct(s, t) for s, t in (outs if many else [outs])]
    return pl.pallas_call(
        kernel,
        out_shape=shapes if many else shapes[0],
        in_specs=[pl.BlockSpec(memory_space=pltpu.VMEM)] * len(args),
        out_specs=(
            [pl.BlockSpec(memory_space=pltpu.VMEM)] * len(shapes)
            if many
            else pl.BlockSpec(memory_space=pltpu.VMEM)
        ),
        scratch_shapes=list(scratch),
        compiler_params=PARAMS,
        name=name,
    )(*args)


def exchange(x, axis):
    return lax.all_to_all(x, axis, 0, 0, tiled=True)


def local(hidden_in, spatial_triple, context_grad, out_weight, triple_weight):
    hidden_in = hidden_in.reshape(TOKENS, D)
    spatial = spatial_triple.reshape(TOKENS, 3 * INNER)
    cotangent = context_grad.reshape(TOKENS, INNER)

    packed = jnp.concatenate([out_weight.T, triple_weight], axis=1)[None]
    packed = lax.all_gather(packed, "fx", axis=0, tiled=True)
    out_copies, triple_rows = call(
        gather_kernel,
        "gather_weights",
        [((GY, 72, INNER), BF), ((72, 3 * INNER), BF)],
        packed,
        scratch=[pltpu.VMEM((72, 4 * INNER), F32)],
    )
    weight = lax.all_gather(triple_rows, "fy", axis=0, tiled=True)
    spatial, hidden_in, cotangent, out_copies = lax.optimization_barrier(
        (spatial, hidden_in, cotangent, out_copies)
    )
    context, hidden_placed = call(
        context_kernel,
        "spatial_context",
        [((TOKENS, INNER), BF), ((TOKENS, D), BF)],
        spatial,
        hidden_in,
        FEATURE_AT[None],
    )
    out_rows = exchange(out_copies, "fy").reshape(D, INNER)
    payload = call(
        hidden_kernel,
        "hidden",
        ((TOKENS, D + INNER), BF),
        context,
        hidden_placed,
        out_rows,
        ROW_AT[:, None],
    )
    payload = exchange(payload.reshape(GY, GX, D + INNER), "fy")
    payload = exchange(jnp.transpose(payload, (1, 0, 2)), "fx").reshape(TOKENS, D + INNER)
    message = call(
        temporal_kernel,
        "temporal_back",
        ((GY, 48, D), BF),
        payload,
        weight,
        cotangent,
        ROW_AT[:, None],
        HALF_A[None],
        HALF_B[None],
    )
    message = exchange(message, "fy")
    message = call(
        turn_kernel,
        "turn",
        ((GX, 24, D), BF),
        message,
        ROW_BACK[:, None],
        FIRST_ROWS[:, None],
        LAST_ROW[:, None],
    )
    message = exchange(message, "fx")
    part = call(sum_kernel, "weight_sum", ((16, INNER), F32), message)
    parts = lax.all_gather(part[None, :ROWS], "dp", axis=0, tiled=True)
    grad_out_weight = (jnp.sum(parts, axis=0) / lax.axis_size("dp")).T
    grad_triple, grad_hidden = call(
        final_kernel,
        "spatial_back",
        [((TOKENS, 3 * INNER), BF), ((TOKENS, D), BF)],
        message,
        out_rows,
        spatial,
        PLACE_OF[None],
    )
    return (
        grad_triple.reshape(1, 1, TOKENS, 3 * INNER),
        grad_hidden.reshape(1, 1, TOKENS, D),
        grad_out_weight,
    )


def solution(mesh):
    placed = (
        P("dp", ("fx", "fy"), None, None),
        P("dp", ("fx", "fy"), None, None),
        P("dp", None, ("fx", "fy"), None),
        P(None, ("fx", "fy")),
        P(("fx", "fy"), None),
    )
    return jax.shard_map(
        local,
        mesh=mesh,
        in_specs=placed,
        out_specs=(
            P("dp", ("fx", "fy"), None, None),
            P("dp", ("fx", "fy"), None, None),
            P(None, ("fx", "fy")),
        ),
        check_vma=False,
    )
```

```python
import math

import numpy as np
import jax
import jax.numpy as jnp
from jax import lax
from jax.experimental import pallas as pl
from jax.experimental.pallas import tpu as pltpu
from jax.sharding import PartitionSpec as P

HEADS = 8
SIZE = 72
INNER = HEADS * SIZE
D = 1152
TOKENS = 128
GX, GY = 8, 16
CLIP_GROUPS = 4
ROWS = 9
PART, REST = 864, 288
BF = jnp.bfloat16
F32 = jnp.float32
SCALE = 1.0 / math.sqrt(SIZE)
PARAMS = pltpu.CompilerParams(vmem_limit_bytes=48 * 1024 * 1024)

_place = np.arange(D)
_j, _i, _r = _place // 72, (_place // 9) % 8, _place % 9
FEATURE_AT = ((_i * GY + _j) * ROWS + _r).astype(np.int32)
PLACE_OF = np.argsort(FEATURE_AT).astype(np.int32)
_t = np.arange(TOKENS)
ROW_AT = ((_t % 8) * 16 + _t // 8).astype(np.int32)
ROW_BACK = ((_t % 16) * 8 + _t // 16).astype(np.int32)


def dot(a, b, dims):
    return lax.dot_general(a, b, (dims, ((), ())), preferred_element_type=F32)


def nn(a, b):
    return dot(a, b, ((1,), (0,)))


def nt(a, b):
    return dot(a, b, ((1,), (1,)))


def tn(a, b):
    return dot(a, b, ((0,), (0,)))


def pick_columns(rows, source):
    at = lax.broadcasted_iota(jnp.int32, (rows, source.shape[1]), 0)
    return jnp.where(at == source, 1.0, 0.0).astype(BF)


def pick_rows(source, columns):
    at = lax.broadcasted_iota(jnp.int32, (source.shape[0], columns), 1)
    return jnp.where(at == source, 1.0, 0.0).astype(BF)


def stack_heads(x):
    lane = lax.broadcasted_iota(jnp.int32, (1, INNER), 1)
    parts = []
    for h in range(HEADS):
        mask = jnp.where((lane >= h * SIZE) & (lane < (h + 1) * SIZE), 1.0, 0.0).astype(BF)
        parts.append(x * mask)
    return jnp.concatenate(parts, axis=0)


def head_of(x, h):
    return x[:, h * TOKENS:(h + 1) * TOKENS]


def softmax(scores):
    shifted = scores * SCALE
    top = jnp.max(shifted, axis=-1, keepdims=True)
    e = jnp.exp(shifted - top)
    return e / jnp.sum(e, axis=-1, keepdims=True)


def attend(q, k, v):
    scores = nt(q, stack_heads(k))
    weights = [softmax(head_of(scores, h)).astype(BF) for h in range(HEADS)]
    return nn(jnp.concatenate(weights, axis=1), stack_heads(v))


def attend_back(q, k, v, cot):
    stacked_k = stack_heads(k)
    scores = nt(q, stacked_k)
    grad_weights = nt(cot, stack_heads(v))
    weights, grad_scores = [], []
    for h in range(HEADS):
        p = softmax(head_of(scores, h))
        g = head_of(grad_weights, h)
        mean = jnp.sum(p * g, axis=-1, keepdims=True)
        weights.append(p.astype(BF))
        grad_scores.append((p * (g - mean) * SCALE).astype(BF))
    grad_q = nn(jnp.concatenate(grad_scores, axis=1), stacked_k)
    grad_k = tn(jnp.concatenate(grad_scores, axis=0), stack_heads(q))
    grad_v = tn(jnp.concatenate(weights, axis=0), stack_heads(cot))
    return grad_q, grad_k, grad_v


def split_triple(triple):
    return triple[:, :INNER], triple[:, INNER:2 * INNER], triple[:, 2 * INNER:]


def spread(x, held):
    for t in range(x.shape[1] // 128):
        held[:, t, :] = x[:, t * 128:(t + 1) * 128]


def collect(held, first, count):
    return jnp.concatenate([held[:, t, :] for t in range(first, first + count)], axis=1)


def context_kernel(triple, hidden_in, tokens, held):
    q, k, v = split_triple(triple[...])
    context = attend(q, k, v)
    blank = jnp.zeros((TOKENS, 16 * 128 - D - INNER), F32)
    spread(jnp.concatenate([hidden_in[...].astype(F32), context, blank], axis=1), held)
    tokens[...] = held[...].astype(BF)


def forward_kernel(core, packed, copies, held):
    for i in range(GX):
        held[i * ROWS:(i + 1) * ROWS, :] = packed[i].astype(F32)
    part = jnp.where(core[0] == 0, held[:, :D], held[:, D:]).astype(BF)
    for j in range(GY):
        copies[j] = part


def place_kernel(core, near, tokens, feature_at, placed, held):
    held[...] = tokens[...].astype(F32)
    hidden_in = collect(held, 0, 9).astype(BF)
    ctx32 = collect(held, 9, 5)[:, :INNER]
    half = jnp.where(core[0] == 0, ctx32[:, :REST], ctx32[:, REST:]).astype(BF)
    placed[...] = nn(hidden_in, pick_columns(D, feature_at[...])) + nt(half, near[:, PART:])


def temporal_kernel(
    core, near, far, placed, tokens, cotangent, row_at, message, out_rows, held
):
    first = core[0] == 0
    w_near = near[...]
    w_far = far[...]
    near_out = w_near[:, PART:]
    far_out = w_far[:, PART:]
    out_rows[:, :REST] = jnp.where(first, near_out, far_out)
    out_rows[:, REST:] = jnp.where(first, far_out, near_out)
    held[...] = tokens[:, 8:, :].astype(F32)
    ctx32 = collect(held, 1, 5)[:, :INNER]
    half = jnp.where(first, ctx32[:, REST:], ctx32[:, :REST]).astype(BF)

    hidden = (placed[...] + nt(half, far_out)).astype(BF).astype(F32)
    centred = hidden - jnp.mean(hidden, axis=-1, keepdims=True)
    scale = lax.rsqrt(jnp.mean(centred * centred, axis=-1, keepdims=True) + 1e-06)
    normal = centred * scale
    normed = normal.astype(BF)
    t_near = nn(normed, w_near)[:, :PART]
    t_far = nn(normed, w_far)[:, :PART]
    triple = jnp.concatenate(
        [jnp.where(first, t_near, t_far), jnp.where(first, t_far, t_near)], axis=1
    ).astype(BF)
    q, k, v = split_triple(triple)
    grads = jnp.concatenate(attend_back(q, k, v, cotangent[...]), axis=1)
    blank = jnp.zeros((TOKENS, REST), F32)
    left = jnp.concatenate([grads[:, :PART], blank], axis=1)
    right = jnp.concatenate([grads[:, PART:], blank], axis=1)
    grad_normal = nt(jnp.where(first, left, right).astype(BF), w_near) + nt(
        jnp.where(first, right, left).astype(BF), w_far
    )
    along = jnp.mean(grad_normal * normal, axis=-1, keepdims=True)
    level = jnp.mean(grad_normal, axis=-1, keepdims=True)
    grad_hidden = (scale * (grad_normal - level - normal * along)).astype(BF)
    turned = nn(pick_rows(row_at[...], TOKENS), grad_hidden)
    low, high = turned[:, :INNER], turned[:, INNER:]
    term = tn(grad_hidden, ctx32.astype(BF))
    for j in range(GY):
        message[j] = jnp.concatenate(
            [
                low[j * 8:(j + 1) * 8],
                high[j * 8:(j + 1) * 8],
                term[j * 72:(j + 1) * 72],
            ],
            axis=0,
        ).astype(BF)


def turn_kernel(received, row_back, message, held):
    one = received[0].astype(F32)
    total, low, high = one[16:], [one[:8]], [one[8:16]]
    for j in range(1, GY):
        one = received[j].astype(F32)
        total = total + one[16:]
        low.append(one[:8])
        high.append(one[8:16])
    held[:72, :] = total
    held[72:, :] = jnp.zeros((8, INNER), F32)
    turn = pick_rows(row_back[...], TOKENS)
    low = nn(turn, jnp.concatenate(low, axis=0).astype(BF)).astype(BF)
    high = nn(turn, jnp.concatenate(high, axis=0).astype(BF)).astype(BF)
    for i in range(GX):
        message[i, :16, :INNER] = low[i * 16:(i + 1) * 16]
        message[i, :16, INNER:] = high[i * 16:(i + 1) * 16]
        at = i * ROWS
        message[i, 16:, :INNER] = held[at:at + 8, :].astype(BF)
        message[i, 16:, INNER:] = held[at + 8:at + 16, :].astype(BF)


def sum_kernel(received, total):
    s = received[0, 16:, :].astype(F32)
    for i in range(1, GX):
        s = s + received[i, 16:, :].astype(F32)
    total[0, :8] = s[:, :INNER]
    total[0, 8:] = s[:1, INNER:]


def final_kernel(received, out_rows, triple, place_of, grad_triple, grad_hidden):
    grad = received[:, :16, :].reshape(TOKENS, D)
    grad_hidden[...] = nn(grad, pick_columns(D, place_of[...])).astype(BF)
    cot = nn(grad, out_rows[...]).astype(BF)
    q, k, v = split_triple(triple[...])
    grad_triple[...] = jnp.concatenate(attend_back(q, k, v, cot), axis=1).astype(BF)


def call(kernel, name, outs, *args, scratch=()):
    many = isinstance(outs, list)
    shapes = [jax.ShapeDtypeStruct(s, t) for s, t in (outs if many else [outs])]
    return pl.pallas_call(
        kernel,
        out_shape=shapes if many else shapes[0],
        in_specs=[
            pl.BlockSpec(memory_space=pltpu.SMEM if a.ndim == 1 else pltpu.VMEM) for a in args
        ],
        out_specs=(
            [pl.BlockSpec(memory_space=pltpu.VMEM)] * len(shapes)
            if many
            else pl.BlockSpec(memory_space=pltpu.VMEM)
        ),
        scratch_shapes=list(scratch),
        compiler_params=PARAMS,
        name=name,
    )(*args)


def exchange(x, axis):
    return lax.all_to_all(x, axis, 0, 0, tiled=True)


def local(hidden_in, spatial_triple, context_grad, out_weight, triple_weight):
    hidden_in = hidden_in.reshape(TOKENS, D)
    spatial = spatial_triple.reshape(TOKENS, 3 * INNER)
    cotangent = context_grad.reshape(TOKENS, INNER)

    core = (lax.axis_index("fx") % 2).astype(jnp.int32)[None]
    out_t = out_weight.T
    packed = jnp.concatenate(
        [triple_weight[:, :PART], out_t[:, :REST], triple_weight[:, PART:], out_t[:, REST:]],
        axis=1,
    )
    packed = lax.all_gather(packed[None], "fx", axis=0, tiled=True)
    slabs = (TOKENS, 16, 128)
    held = pltpu.VMEM(slabs, F32)
    tokens = call(
        context_kernel, "spatial_context", (slabs, BF), spatial, hidden_in, scratch=[held]
    )
    tokens = exchange(tokens, ("fx", "fy"))
    packed, tokens = lax.optimization_barrier((packed, tokens))
    near = call(
        forward_kernel,
        "forward",
        ((GY, 72, D), BF),
        core,
        packed,
        scratch=[pltpu.VMEM((72, 2 * D), F32)],
    )
    near = exchange(near, "fy").reshape(D, D)
    far = lax.ppermute(near, "fx", [(i, i ^ 1) for i in range(GX)])
    placed = call(
        place_kernel,
        "hidden_near",
        ((TOKENS, D), F32),
        core,
        near,
        tokens,
        FEATURE_AT[None],
        scratch=[held],
    )
    message, out_rows = call(
        temporal_kernel,
        "temporal_back",
        [((GY, 88, INNER), BF), ((D, INNER), BF)],
        core,
        near,
        far,
        placed,
        tokens,
        cotangent,
        ROW_AT[:, None],
        scratch=[pltpu.VMEM((TOKENS, 8, 128), F32)],
    )
    message = exchange(message, "fy")
    message = call(
        turn_kernel,
        "turn",
        ((GX, 24, D), BF),
        message,
        ROW_BACK[:, None],
        scratch=[pltpu.VMEM((80, INNER), F32)],
    )
    message = exchange(message, "fx")
    total = call(sum_kernel, "weight_sum", ((1, ROWS, INNER), F32), message)
    totals = lax.all_gather(total, "dp", axis=0, tiled=True)
    grad_triple, grad_hidden = call(
        final_kernel,
        "spatial_back",
        [((TOKENS, 3 * INNER), BF), ((TOKENS, D), BF)],
        message,
        out_rows,
        spatial,
        PLACE_OF[None],
    )
    grad_out_weight = (jnp.sum(totals, axis=0) / CLIP_GROUPS).T
    return (
        grad_triple.reshape(1, 1, TOKENS, 3 * INNER),
        grad_hidden.reshape(1, 1, TOKENS, D),
        grad_out_weight,
    )


def solution(mesh):
    placed = (
        P("dp", ("fx", "fy"), None, None),
        P("dp", ("fx", "fy"), None, None),
        P("dp", None, ("fx", "fy"), None),
        P(None, ("fx", "fy")),
        P(("fx", "fy"), None),
    )
    return jax.shard_map(
        local,
        mesh=mesh,
        in_specs=placed,
        out_specs=(
            P("dp", ("fx", "fy"), None, None),
            P("dp", ("fx", "fy"), None, None),
            P(None, ("fx", "fy")),
        ),
        check_vma=False,
    )
```

```python
import math

import numpy as np
import jax
import jax.numpy as jnp
from jax import lax
from jax.experimental import pallas as pl
from jax.experimental.pallas import tpu as pltpu
from jax.sharding import PartitionSpec as P

HEADS = 8
SIZE = 72
INNER = HEADS * SIZE
D = 1152
TOKENS = 128
GX, GY = 8, 16
CLIP_GROUPS = 4
ROWS = 9
PART, REST = 864, 288
BF = jnp.bfloat16
F32 = jnp.float32
SCALE = 1.0 / math.sqrt(SIZE)
PARAMS = pltpu.CompilerParams(vmem_limit_bytes=48 * 1024 * 1024)

_place = np.arange(D)
_j, _i, _r = _place // 72, (_place // 9) % 8, _place % 9
FEATURE_AT = ((_i * GY + _j) * ROWS + _r).astype(np.int32)
PLACE_OF = np.argsort(FEATURE_AT).astype(np.int32)


def dot(a, b, dims):
    return lax.dot_general(a, b, (dims, ((), ())), preferred_element_type=F32)


def nn(a, b):
    return dot(a, b, ((1,), (0,)))


def nt(a, b):
    return dot(a, b, ((1,), (1,)))


def tn(a, b):
    return dot(a, b, ((0,), (0,)))


def pick_columns(rows, source):
    at = lax.broadcasted_iota(jnp.int32, (rows, source.shape[1]), 0)
    return jnp.where(at == source, 1.0, 0.0).astype(BF)


def turn_rows(minor):
    row = lax.broadcasted_iota(jnp.int32, (TOKENS, TOKENS), 0)
    column = lax.broadcasted_iota(jnp.int32, (TOKENS, TOKENS), 1)
    shift = minor.bit_length() - 1
    source = (row & (minor - 1)) * (TOKENS // minor) + (row >> shift)
    return jnp.where(column == source, 1.0, 0.0).astype(BF)


def stack_heads(x):
    lane = lax.broadcasted_iota(jnp.int32, (1, INNER), 1)
    parts = []
    for h in range(HEADS):
        mask = jnp.where((lane >= h * SIZE) & (lane < (h + 1) * SIZE), 1.0, 0.0).astype(BF)
        parts.append(x * mask)
    return jnp.concatenate(parts, axis=0)


def head_of(x, h):
    return x[:, h * TOKENS:(h + 1) * TOKENS]


def softmax(scores):
    shifted = scores * SCALE
    top = jnp.max(shifted, axis=-1, keepdims=True)
    e = jnp.exp(shifted - top)
    return e / jnp.sum(e, axis=-1, keepdims=True)


def stack_heads_turned(x):
    row = lax.broadcasted_iota(jnp.int32, (INNER, 1), 0)
    parts = []
    for h in range(HEADS):
        mask = jnp.where((row >= h * SIZE) & (row < (h + 1) * SIZE), 1.0, 0.0).astype(BF)
        parts.append(x * mask)
    return jnp.concatenate(parts, axis=1)


def attend_turned(q, k, v):
    scores = tn(q, stack_heads_turned(k))
    weights = [softmax(head_of(scores, h)).astype(BF) for h in range(HEADS)]
    return nt(jnp.concatenate(weights, axis=1), stack_heads_turned(v))


def attend_back_turned(q, k, v, cot):
    stacked_k = stack_heads_turned(k)
    scores = tn(q, stacked_k)
    grad_weights = nn(cot.astype(BF), stack_heads_turned(v))
    weights, grad_scores = softmax_back(scores, grad_weights)
    grad_q = nt(stacked_k, jnp.concatenate(grad_scores, axis=1))
    grad_k = nn(stack_heads_turned(q), jnp.concatenate(grad_scores, axis=0))
    cot_turned = jnp.transpose(cot).astype(BF)
    grad_v = nn(stack_heads_turned(cot_turned), jnp.concatenate(weights, axis=0))
    return grad_q, grad_k, grad_v


def softmax_back(scores, grad_weights):
    weights, grad_scores = [], []
    for h in range(HEADS):
        p = softmax(head_of(scores, h))
        g = head_of(grad_weights, h)
        mean = jnp.sum(p * g, axis=-1, keepdims=True)
        weights.append(p.astype(BF))
        grad_scores.append((p * (g - mean) * SCALE).astype(BF))
    return weights, grad_scores


def attend_back(q, k, v, cot):
    stacked_k = stack_heads(k)
    scores = nt(q, stacked_k)
    grad_weights = nt(cot, stack_heads(v))
    weights, grad_scores = softmax_back(scores, grad_weights)
    grad_q = nn(jnp.concatenate(grad_scores, axis=1), stacked_k)
    grad_k = tn(jnp.concatenate(grad_scores, axis=0), stack_heads(q))
    grad_v = tn(jnp.concatenate(weights, axis=0), stack_heads(cot))
    return grad_q, grad_k, grad_v


def split_triple(triple):
    return triple[:, :INNER], triple[:, INNER:2 * INNER], triple[:, 2 * INNER:]


def spread(x, held):
    for t in range(x.shape[1] // 128):
        held[:, t, :] = x[:, t * 128:(t + 1) * 128]


def collect(held, first, count):
    return jnp.concatenate([held[:, t, :] for t in range(first, first + count)], axis=1)


def context_kernel(triple, hidden_there, tokens, held, hidden_in, arrived):
    fetch = pltpu.make_async_copy(hidden_there, hidden_in, arrived)
    fetch.start()
    context = attend_turned(
        triple[:INNER, :], triple[INNER:2 * INNER, :], triple[2 * INNER:, :]
    )
    blank = jnp.zeros((TOKENS, 16 * 128 - D - INNER), F32)
    fetch.wait()
    spread(jnp.concatenate([hidden_in[...].astype(F32), context, blank], axis=1), held)
    tokens[...] = held[...].astype(BF)


def forward_kernel(core, packed, copies, held):
    for i in range(GX):
        held[i * ROWS:(i + 1) * ROWS, :] = packed[i].astype(F32)
    part = jnp.where(core[0] == 0, held[:, :D], held[:, D:]).astype(BF)
    for j in range(GY):
        copies[j] = part


def place_kernel(core, near, tokens, feature_at, placed, near_copy, held):
    held[...] = tokens[...].astype(F32)
    hidden_in = collect(held, 0, 9).astype(BF)
    ctx32 = collect(held, 9, 5)[:, :INNER]
    half = jnp.where(core[0] == 0, ctx32[:, :REST], ctx32[:, REST:]).astype(BF)
    near_copy[...] = near[...]
    mixed = jnp.transpose(nt(near[:, PART:], half))
    placed[...] = nn(hidden_in, pick_columns(D, feature_at[...])) + mixed


def temporal_kernel(
    core, near, far, placed, tokens, cotangent, message, out_rows, held
):
    first = core[0] == 0
    w_near = near[...]
    w_far = far[...]
    near_out = w_near[:, PART:]
    far_out = w_far[:, PART:]
    out_rows[:, :REST] = jnp.where(first, near_out, far_out)
    out_rows[:, REST:] = jnp.where(first, far_out, near_out)
    held[...] = tokens[:, 8:, :].astype(F32)
    ctx32 = collect(held, 1, 5)[:, :INNER]
    half = jnp.where(first, ctx32[:, REST:], ctx32[:, :REST]).astype(BF)

    hidden = (placed[...] + jnp.transpose(nt(far_out, half))).astype(BF).astype(F32)
    centred = hidden - jnp.mean(hidden, axis=-1, keepdims=True)
    scale = lax.rsqrt(jnp.mean(centred * centred, axis=-1, keepdims=True) + 1e-06)
    normal = centred * scale
    normed = normal.astype(BF)
    t_near = nn(normed, w_near)[:, :PART]
    t_far = nn(normed, w_far)[:, :PART]
    triple = jnp.concatenate(
        [jnp.where(first, t_near, t_far), jnp.where(first, t_far, t_near)], axis=1
    ).astype(BF)
    q, k, v = split_triple(triple)
    grads = jnp.concatenate(attend_back(q, k, v, cotangent[...]), axis=1)
    blank = jnp.zeros((TOKENS, REST), F32)
    left = jnp.concatenate([grads[:, :PART], blank], axis=1)
    right = jnp.concatenate([grads[:, PART:], blank], axis=1)
    grad_normal = jnp.transpose(
        nt(w_near, jnp.where(first, left, right).astype(BF))
        + nt(w_far, jnp.where(first, right, left).astype(BF))
    )
    along = jnp.mean(grad_normal * normal, axis=-1, keepdims=True)
    level = jnp.mean(grad_normal, axis=-1, keepdims=True)
    grad_hidden = (scale * (grad_normal - level - normal * along)).astype(BF)
    turned = nn(turn_rows(GX), grad_hidden)
    low, high = turned[:, :INNER], turned[:, INNER:]
    term = tn(grad_hidden, ctx32.astype(BF))
    for j in range(GY):
        message[j] = jnp.concatenate(
            [
                low[j * 8:(j + 1) * 8],
                high[j * 8:(j + 1) * 8],
                term[j * 72:(j + 1) * 72],
            ],
            axis=0,
        ).astype(BF)


def turn_kernel(received, message, held):
    one = received[0].astype(F32)
    total, low, high = one[16:], [one[:8]], [one[8:16]]
    for j in range(1, GY):
        one = received[j].astype(F32)
        total = total + one[16:]
        low.append(one[:8])
        high.append(one[8:16])
    held[:72, :] = total
    held[72:, :] = jnp.zeros((8, INNER), F32)
    turn = turn_rows(GY)
    low = nn(turn, jnp.concatenate(low, axis=0).astype(BF)).astype(BF)
    high = nn(turn, jnp.concatenate(high, axis=0).astype(BF)).astype(BF)
    for i in range(GX):
        message[i, :16, :INNER] = low[i * 16:(i + 1) * 16]
        message[i, :16, INNER:] = high[i * 16:(i + 1) * 16]
        at = i * ROWS
        message[i, 16:, :INNER] = held[at:at + 8, :].astype(BF)
        message[i, 16:, INNER:] = held[at + 8:at + 16, :].astype(BF)


def sum_kernel(received, total):
    s = received[0, 16:, :].astype(F32)
    for i in range(1, GX):
        s = s + received[i, 16:, :].astype(F32)
    total[0, :8] = s[:, :INNER]
    total[0, 8:] = s[:1, INNER:]


def final_kernel(received, out_rows, triple, place_of, grad_triple, grad_hidden):
    grad = received[:, :16, :].reshape(TOKENS, D)
    grad_hidden[...] = nn(grad, pick_columns(D, place_of[...])).astype(BF)
    grads = attend_back_turned(
        triple[:INNER, :],
        triple[INNER:2 * INNER, :],
        triple[2 * INNER:, :],
        nn(grad, out_rows[...]),
    )
    for n, part in enumerate(grads):
        grad_triple[n * INNER:(n + 1) * INNER, :] = part.astype(BF)


def call(kernel, name, outs, *args, scratch=(), there=()):
    many = isinstance(outs, list)
    shapes = [jax.ShapeDtypeStruct(s, t) for s, t in (outs if many else [outs])]
    return pl.pallas_call(
        kernel,
        out_shape=shapes if many else shapes[0],
        in_specs=[
            pl.BlockSpec(
                memory_space=pl.ANY if n in there else pltpu.SMEM if a.ndim == 1 else pltpu.VMEM
            )
            for n, a in enumerate(args)
        ],
        out_specs=(
            [pl.BlockSpec(memory_space=pltpu.VMEM)] * len(shapes)
            if many
            else pl.BlockSpec(memory_space=pltpu.VMEM)
        ),
        scratch_shapes=list(scratch),
        compiler_params=PARAMS,
        name=name,
    )(*args)


def exchange(x, axis):
    return lax.all_to_all(x, axis, 0, 0, tiled=True)


def local(hidden_in, spatial_triple, context_grad, out_weight, triple_weight):
    hidden_in = hidden_in.reshape(TOKENS, D)
    spatial = spatial_triple.reshape(TOKENS, 3 * INNER).T
    cotangent = context_grad.reshape(TOKENS, INNER)

    core = (lax.axis_index("fx") % 2).astype(jnp.int32)[None]
    out_t = out_weight.T
    packed = jnp.concatenate(
        [triple_weight[:, :PART], out_t[:, :REST], triple_weight[:, PART:], out_t[:, REST:]],
        axis=1,
    )
    packed = lax.all_gather(packed[None], "fx", axis=0, tiled=True)
    slabs = (TOKENS, 16, 128)
    held = pltpu.VMEM(slabs, F32)
    tokens = call(
        context_kernel,
        "spatial_context",
        (slabs, BF),
        spatial,
        hidden_in,
        scratch=[held, pltpu.VMEM((TOKENS, D), BF), pltpu.SemaphoreType.DMA],
        there=(1,),
    )
    tokens = exchange(tokens, ("fx", "fy"))
    packed, tokens = lax.optimization_barrier((packed, tokens))
    near = call(
        forward_kernel,
        "forward",
        ((GY, 72, D), BF),
        core,
        packed,
        scratch=[pltpu.VMEM((72, 2 * D), F32)],
    )
    near = exchange(near, "fy").reshape(D, D)
    far = lax.ppermute(near, "fx", [(i, i ^ 1) for i in range(GX)])
    placed, near = call(
        place_kernel,
        "hidden_near",
        [((TOKENS, D), F32), ((D, D), BF)],
        core,
        near,
        tokens,
        FEATURE_AT[None],
        scratch=[held],
    )
    message, out_rows = call(
        temporal_kernel,
        "temporal_back",
        [((GY, 88, INNER), BF), ((D, INNER), BF)],
        core,
        near,
        far,
        placed,
        tokens,
        cotangent,
        scratch=[pltpu.VMEM((TOKENS, 8, 128), F32)],
    )
    message = exchange(message, "fy")
    message = call(
        turn_kernel,
        "turn",
        ((GX, 24, D), BF),
        message,
        scratch=[pltpu.VMEM((80, INNER), F32)],
    )
    message = exchange(message, "fx")
    total = call(sum_kernel, "weight_sum", ((1, ROWS, INNER), F32), message)
    totals = lax.all_gather(total, "dp", axis=0, tiled=True)
    grad_triple, grad_hidden = call(
        final_kernel,
        "spatial_back",
        [((3 * INNER, TOKENS), BF), ((TOKENS, D), BF)],
        message,
        out_rows,
        spatial,
        PLACE_OF[None],
    )
    grad_out_weight = (jnp.sum(totals, axis=0) / CLIP_GROUPS).T
    return (
        grad_triple.T.reshape(1, 1, TOKENS, 3 * INNER),
        grad_hidden.reshape(1, 1, TOKENS, D),
        grad_out_weight,
    )


def solution(mesh):
    placed = (
        P("dp", ("fx", "fy"), None, None),
        P("dp", ("fx", "fy"), None, None),
        P("dp", None, ("fx", "fy"), None),
        P(None, ("fx", "fy")),
        P(("fx", "fy"), None),
    )
    return jax.shard_map(
        local,
        mesh=mesh,
        in_specs=placed,
        out_specs=(
            P("dp", ("fx", "fy"), None, None),
            P("dp", ("fx", "fy"), None, None),
            P(None, ("fx", "fy")),
        ),
        check_vma=False,
    )
```

```python
import math

import numpy as np
import jax
import jax.numpy as jnp
from jax import lax
from jax.experimental import pallas as pl
from jax.experimental.pallas import tpu as pltpu
from jax.sharding import PartitionSpec as P

HEADS = 8
SIZE = 72
INNER = HEADS * SIZE
D = 1152
TOKENS = 128
GX, GY = 8, 16
CLIP_GROUPS = 4
ROWS = 9
PART, REST = 864, 288
BF = jnp.bfloat16
F32 = jnp.float32
SCALE = 1.0 / math.sqrt(SIZE)
PARAMS = pltpu.CompilerParams(vmem_limit_bytes=48 * 1024 * 1024)

_place = np.arange(D)
_j, _i, _r = _place // 72, (_place // 9) % 8, _place % 9
FEATURE_AT = ((_i * GY + _j) * ROWS + _r).astype(np.int32)
PLACE_OF = np.argsort(FEATURE_AT).astype(np.int32)


def dot(a, b, dims):
    return lax.dot_general(a, b, (dims, ((), ())), preferred_element_type=F32)


def nn(a, b):
    return dot(a, b, ((1,), (0,)))


def nt(a, b):
    return dot(a, b, ((1,), (1,)))


def tn(a, b):
    return dot(a, b, ((0,), (0,)))


def pick_columns(rows, source):
    at = lax.broadcasted_iota(jnp.int32, (rows, source.shape[1]), 0)
    return jnp.where(at == source, 1.0, 0.0).astype(BF)


def turn_rows(minor):
    row = lax.broadcasted_iota(jnp.int32, (TOKENS, TOKENS), 0)
    column = lax.broadcasted_iota(jnp.int32, (TOKENS, TOKENS), 1)
    shift = minor.bit_length() - 1
    source = (row & (minor - 1)) * (TOKENS // minor) + (row >> shift)
    return jnp.where(column == source, 1.0, 0.0).astype(BF)


def stack_heads(x):
    lane = lax.broadcasted_iota(jnp.int32, (1, INNER), 1)
    parts = []
    for h in range(HEADS):
        mask = jnp.where((lane >= h * SIZE) & (lane < (h + 1) * SIZE), 1.0, 0.0).astype(BF)
        parts.append(x * mask)
    return jnp.concatenate(parts, axis=0)


def head_of(x, h):
    return x[:, h * TOKENS:(h + 1) * TOKENS]


def softmax(scores):
    shifted = scores * SCALE
    top = jnp.max(shifted, axis=-1, keepdims=True)
    e = jnp.exp(shifted - top)
    return e / jnp.sum(e, axis=-1, keepdims=True)


def stack_heads_turned(x):
    row = lax.broadcasted_iota(jnp.int32, (INNER, 1), 0)
    parts = []
    for h in range(HEADS):
        mask = jnp.where((row >= h * SIZE) & (row < (h + 1) * SIZE), 1.0, 0.0).astype(BF)
        parts.append(x * mask)
    return jnp.concatenate(parts, axis=1)


def attend_turned(q, k, v):
    scores = tn(q, stack_heads_turned(k))
    weights = [softmax(head_of(scores, h)).astype(BF) for h in range(HEADS)]
    return nt(jnp.concatenate(weights, axis=1), stack_heads_turned(v))


def attend_back_turned(q, k, v, cot):
    stacked_k = stack_heads_turned(k)
    scores = tn(q, stacked_k)
    grad_weights = nn(cot.astype(BF), stack_heads_turned(v))
    weights, grad_scores = softmax_back(scores, grad_weights)
    grad_q = nt(stacked_k, jnp.concatenate(grad_scores, axis=1))
    grad_k = nn(stack_heads_turned(q), jnp.concatenate(grad_scores, axis=0))
    cot_turned = jnp.transpose(cot).astype(BF)
    grad_v = nn(stack_heads_turned(cot_turned), jnp.concatenate(weights, axis=0))
    return grad_q, grad_k, grad_v


def softmax_back(scores, grad_weights):
    weights, grad_scores = [], []
    for h in range(HEADS):
        p = softmax(head_of(scores, h))
        g = head_of(grad_weights, h)
        mean = jnp.sum(p * g, axis=-1, keepdims=True)
        weights.append(p.astype(BF))
        grad_scores.append((p * (g - mean) * SCALE).astype(BF))
    return weights, grad_scores


def attend_back(q, k, v, cot):
    stacked_k = stack_heads(k)
    scores = nt(q, stacked_k)
    grad_weights = nt(cot, stack_heads(v))
    weights, grad_scores = softmax_back(scores, grad_weights)
    grad_q = nn(jnp.concatenate(grad_scores, axis=1), stacked_k)
    grad_k = tn(jnp.concatenate(grad_scores, axis=0), stack_heads(q))
    grad_v = tn(jnp.concatenate(weights, axis=0), stack_heads(cot))
    return grad_q, grad_k, grad_v


def split_triple(triple):
    return triple[:, :INNER], triple[:, INNER:2 * INNER], triple[:, 2 * INNER:]


def spread(x, held):
    for t in range(x.shape[1] // 128):
        held[:, t, :] = x[:, t * 128:(t + 1) * 128]


def collect(held, first, count):
    return jnp.concatenate([held[:, t, :] for t in range(first, first + count)], axis=1)


def context_kernel(triple, hidden_in, tokens, held):
    context = attend_turned(
        triple[:INNER, :], triple[INNER:2 * INNER, :], triple[2 * INNER:, :]
    )
    blank = jnp.zeros((TOKENS, 16 * 128 - D - INNER), F32)
    spread(jnp.concatenate([hidden_in[...].astype(F32), context, blank], axis=1), held)
    tokens[...] = held[...].astype(BF)


def forward_kernel(core, packed, copies, held):
    for i in range(GX):
        held[i * ROWS:(i + 1) * ROWS, :] = packed[i].astype(F32)
    part = jnp.where(core[0] == 0, held[:, :D], held[:, D:]).astype(BF)
    for j in range(GY):
        copies[j] = part


def place_kernel(core, near, tokens, feature_at, placed, held):
    held[...] = tokens[...].astype(F32)
    hidden_in = collect(held, 0, 9).astype(BF)
    ctx32 = collect(held, 9, 5)[:, :INNER]
    half = jnp.where(core[0] == 0, ctx32[:, :REST], ctx32[:, REST:]).astype(BF)
    mixed = jnp.transpose(nt(near[:, PART:], half))
    placed[...] = nn(hidden_in, pick_columns(D, feature_at[...])) + mixed


def temporal_kernel(
    core, near, far, placed, tokens, cotangent, message, out_rows, held
):
    first = core[0] == 0
    w_near = near[...]
    w_far = far[...]
    near_out = w_near[:, PART:]
    far_out = w_far[:, PART:]
    out_rows[:, :REST] = jnp.where(first, near_out, far_out)
    out_rows[:, REST:] = jnp.where(first, far_out, near_out)
    held[...] = tokens[:, 8:, :].astype(F32)
    ctx32 = collect(held, 1, 5)[:, :INNER]
    half = jnp.where(first, ctx32[:, REST:], ctx32[:, :REST]).astype(BF)

    hidden = (placed[...] + jnp.transpose(nt(far_out, half))).astype(BF).astype(F32)
    centred = hidden - jnp.mean(hidden, axis=-1, keepdims=True)
    scale = lax.rsqrt(jnp.mean(centred * centred, axis=-1, keepdims=True) + 1e-06)
    normal = centred * scale
    normed = normal.astype(BF)
    t_near = nn(normed, w_near)[:, :PART]
    t_far = nn(normed, w_far)[:, :PART]
    triple = jnp.concatenate(
        [jnp.where(first, t_near, t_far), jnp.where(first, t_far, t_near)], axis=1
    ).astype(BF)
    q, k, v = split_triple(triple)
    grads = jnp.concatenate(attend_back(q, k, v, cotangent[...]), axis=1)
    blank = jnp.zeros((TOKENS, REST), F32)
    left = jnp.concatenate([grads[:, :PART], blank], axis=1)
    right = jnp.concatenate([grads[:, PART:], blank], axis=1)
    grad_normal = jnp.transpose(
        nt(w_near, jnp.where(first, left, right).astype(BF))
        + nt(w_far, jnp.where(first, right, left).astype(BF))
    )
    along = jnp.mean(grad_normal * normal, axis=-1, keepdims=True)
    level = jnp.mean(grad_normal, axis=-1, keepdims=True)
    grad_hidden = (scale * (grad_normal - level - normal * along)).astype(BF)
    turned = nn(turn_rows(GX), grad_hidden)
    low, high = turned[:, :INNER], turned[:, INNER:]
    term = tn(grad_hidden, ctx32.astype(BF))
    for j in range(GY):
        message[j] = jnp.concatenate(
            [
                low[j * 8:(j + 1) * 8],
                high[j * 8:(j + 1) * 8],
                term[j * 72:(j + 1) * 72],
            ],
            axis=0,
        ).astype(BF)


def turn_kernel(received, message, held):
    one = received[0].astype(F32)
    total, low, high = one[16:], [one[:8]], [one[8:16]]
    for j in range(1, GY):
        one = received[j].astype(F32)
        total = total + one[16:]
        low.append(one[:8])
        high.append(one[8:16])
    held[:72, :] = total
    held[72:, :] = jnp.zeros((8, INNER), F32)
    turn = turn_rows(GY)
    low = nn(turn, jnp.concatenate(low, axis=0).astype(BF)).astype(BF)
    high = nn(turn, jnp.concatenate(high, axis=0).astype(BF)).astype(BF)
    for i in range(GX):
        message[i, :16, :INNER] = low[i * 16:(i + 1) * 16]
        message[i, :16, INNER:] = high[i * 16:(i + 1) * 16]
        at = i * ROWS
        message[i, 16:, :INNER] = held[at:at + 8, :].astype(BF)
        message[i, 16:, INNER:] = held[at + 8:at + 16, :].astype(BF)


def sum_kernel(received, total):
    s = received[0, 16:, :].astype(F32)
    for i in range(1, GX):
        s = s + received[i, 16:, :].astype(F32)
    total[0, :8] = s[:, :INNER]
    total[0, 8:] = s[:1, INNER:]


def final_kernel(received, out_rows, triple, place_of, grad_triple, grad_hidden):
    grad = received[:, :16, :].reshape(TOKENS, D)
    grad_hidden[...] = nn(grad, pick_columns(D, place_of[...])).astype(BF)
    grads = attend_back_turned(
        triple[:INNER, :],
        triple[INNER:2 * INNER, :],
        triple[2 * INNER:, :],
        nn(grad, out_rows[...]),
    )
    for n, part in enumerate(grads):
        grad_triple[n * INNER:(n + 1) * INNER, :] = part.astype(BF)


def call(kernel, name, outs, *args, scratch=()):
    many = isinstance(outs, list)
    shapes = [jax.ShapeDtypeStruct(s, t) for s, t in (outs if many else [outs])]
    return pl.pallas_call(
        kernel,
        out_shape=shapes if many else shapes[0],
        in_specs=[
            pl.BlockSpec(memory_space=pltpu.SMEM if a.ndim == 1 else pltpu.VMEM) for a in args
        ],
        out_specs=(
            [pl.BlockSpec(memory_space=pltpu.VMEM)] * len(shapes)
            if many
            else pl.BlockSpec(memory_space=pltpu.VMEM)
        ),
        scratch_shapes=list(scratch),
        compiler_params=PARAMS,
        name=name,
    )(*args)


def exchange(x, axis):
    return lax.all_to_all(x, axis, 0, 0, tiled=True)


def local(hidden_in, spatial_triple, context_grad, out_weight, triple_weight):
    hidden_in = hidden_in.reshape(TOKENS, D)
    spatial = spatial_triple.reshape(TOKENS, 3 * INNER).T
    cotangent = context_grad.reshape(TOKENS, INNER)

    core = (lax.axis_index("fx") % 2).astype(jnp.int32)[None]
    out_t = out_weight.T
    packed = jnp.concatenate(
        [triple_weight[:, :PART], out_t[:, :REST], triple_weight[:, PART:], out_t[:, REST:]],
        axis=1,
    )
    packed = lax.all_gather(packed[None], "fx", axis=0, tiled=True)
    slabs = (TOKENS, 16, 128)
    held = pltpu.VMEM(slabs, F32)
    tokens = call(
        context_kernel,
        "spatial_context",
        (slabs, BF),
        spatial,
        hidden_in,
        scratch=[held],
    )
    tokens = exchange(tokens, ("fx", "fy"))
    packed, tokens = lax.optimization_barrier((packed, tokens))
    near = call(
        forward_kernel,
        "forward",
        ((GY, 72, D), BF),
        core,
        packed,
        scratch=[pltpu.VMEM((72, 2 * D), F32)],
    )
    near = exchange(near, "fy").reshape(D, D)
    far = lax.ppermute(near, "fx", [(i, i ^ 1) for i in range(GX)])
    placed = call(
        place_kernel,
        "hidden_near",
        ((TOKENS, D), F32),
        core,
        near,
        tokens,
        FEATURE_AT[None],
        scratch=[held],
    )
    message, out_rows = call(
        temporal_kernel,
        "temporal_back",
        [((GY, 88, INNER), BF), ((D, INNER), BF)],
        core,
        near,
        far,
        placed,
        tokens,
        cotangent,
        scratch=[pltpu.VMEM((TOKENS, 8, 128), F32)],
    )
    message = exchange(message, "fy")
    message = call(
        turn_kernel,
        "turn",
        ((GX, 24, D), BF),
        message,
        scratch=[pltpu.VMEM((80, INNER), F32)],
    )
    message = exchange(message, "fx")
    total = call(sum_kernel, "weight_sum", ((1, ROWS, INNER), F32), message)
    totals = lax.all_gather(total, "dp", axis=0, tiled=True)
    grad_triple, grad_hidden = call(
        final_kernel,
        "spatial_back",
        [((3 * INNER, TOKENS), BF), ((TOKENS, D), BF)],
        message,
        out_rows,
        spatial,
        PLACE_OF[None],
    )
    grad_out_weight = (jnp.sum(totals, axis=0) / CLIP_GROUPS).T
    return (
        grad_triple.T.reshape(1, 1, TOKENS, 3 * INNER),
        grad_hidden.reshape(1, 1, TOKENS, D),
        grad_out_weight,
    )


def solution(mesh):
    placed = (
        P("dp", ("fx", "fy"), None, None),
        P("dp", ("fx", "fy"), None, None),
        P("dp", None, ("fx", "fy"), None),
        P(None, ("fx", "fy")),
        P(("fx", "fy"), None),
    )
    return jax.shard_map(
        local,
        mesh=mesh,
        in_specs=placed,
        out_specs=(
            P("dp", ("fx", "fy"), None, None),
            P("dp", ("fx", "fy"), None, None),
            P(None, ("fx", "fy")),
        ),
        check_vma=False,
    )
```

```python
import math

import numpy as np
import jax
import jax.numpy as jnp
from jax import lax
from jax.experimental import pallas as pl
from jax.experimental.pallas import tpu as pltpu
from jax.sharding import PartitionSpec as P

HEADS = 8
SIZE = 72
INNER = HEADS * SIZE
D = 1152
TOKENS = 128
GX, GY = 8, 16
CLIP_GROUPS = 4
ROWS = 9
PART, REST = 864, 288
BF = jnp.bfloat16
F32 = jnp.float32
SCALE = 1.0 / math.sqrt(SIZE)
PARAMS = pltpu.CompilerParams(vmem_limit_bytes=48 * 1024 * 1024)

_place = np.arange(D)
_j, _i, _r = _place // 72, (_place // 9) % 8, _place % 9
FEATURE_AT = ((_i * GY + _j) * ROWS + _r).astype(np.int32)
PLACE_OF = np.argsort(FEATURE_AT).astype(np.int32)


def dot(a, b, dims):
    return lax.dot_general(a, b, (dims, ((), ())), preferred_element_type=F32)


def nn(a, b):
    return dot(a, b, ((1,), (0,)))


def nt(a, b):
    return dot(a, b, ((1,), (1,)))


def tn(a, b):
    return dot(a, b, ((0,), (0,)))


def pick_columns(rows, source):
    at = lax.broadcasted_iota(jnp.int32, (rows, source.shape[1]), 0)
    return jnp.where(at == source, 1.0, 0.0).astype(BF)


def turn_rows(minor):
    row = lax.broadcasted_iota(jnp.int32, (TOKENS, TOKENS), 0)
    column = lax.broadcasted_iota(jnp.int32, (TOKENS, TOKENS), 1)
    shift = minor.bit_length() - 1
    source = (row & (minor - 1)) * (TOKENS // minor) + (row >> shift)
    return jnp.where(column == source, 1.0, 0.0).astype(BF)


def stack_heads(x):
    lane = lax.broadcasted_iota(jnp.int32, (1, INNER), 1)
    parts = []
    for h in range(HEADS):
        mask = jnp.where((lane >= h * SIZE) & (lane < (h + 1) * SIZE), 1.0, 0.0).astype(BF)
        parts.append(x * mask)
    return jnp.concatenate(parts, axis=0)


def head_of(x, h):
    return x[:, h * TOKENS:(h + 1) * TOKENS]


def softmax(scores):
    shifted = scores * SCALE
    top = jnp.max(shifted, axis=-1, keepdims=True)
    e = jnp.exp(shifted - top)
    return e / jnp.sum(e, axis=-1, keepdims=True)


def stack_heads_turned(x):
    row = lax.broadcasted_iota(jnp.int32, (INNER, 1), 0)
    parts = []
    for h in range(HEADS):
        mask = jnp.where((row >= h * SIZE) & (row < (h + 1) * SIZE), 1.0, 0.0).astype(BF)
        parts.append(x * mask)
    return jnp.concatenate(parts, axis=1)


def attend_turned(q, k, v):
    scores = tn(q, stack_heads_turned(k))
    weights = [softmax(head_of(scores, h)).astype(BF) for h in range(HEADS)]
    return nt(jnp.concatenate(weights, axis=1), stack_heads_turned(v))


def attend_back_turned(q, k, v, cot):
    stacked_k = stack_heads_turned(k)
    scores = tn(q, stacked_k)
    grad_weights = nn(cot.astype(BF), stack_heads_turned(v))
    weights, grad_scores = softmax_back(scores, grad_weights)
    grad_q = nt(stacked_k, jnp.concatenate(grad_scores, axis=1))
    grad_k = nn(stack_heads_turned(q), jnp.concatenate(grad_scores, axis=0))
    cot_turned = jnp.transpose(cot).astype(BF)
    grad_v = nn(stack_heads_turned(cot_turned), jnp.concatenate(weights, axis=0))
    return grad_q, grad_k, grad_v


def softmax_back(scores, grad_weights):
    weights, grad_scores = [], []
    for h in range(HEADS):
        p = softmax(head_of(scores, h))
        g = head_of(grad_weights, h)
        mean = jnp.sum(p * g, axis=-1, keepdims=True)
        weights.append(p.astype(BF))
        grad_scores.append((p * (g - mean) * SCALE).astype(BF))
    return weights, grad_scores


def attend_back(q, k, v, cot):
    stacked_k = stack_heads(k)
    scores = nt(q, stacked_k)
    grad_weights = nt(cot, stack_heads(v))
    weights, grad_scores = softmax_back(scores, grad_weights)
    grad_q = nn(jnp.concatenate(grad_scores, axis=1), stacked_k)
    grad_k = tn(jnp.concatenate(grad_scores, axis=0), stack_heads(q))
    grad_v = tn(jnp.concatenate(weights, axis=0), stack_heads(cot))
    return grad_q, grad_k, grad_v


def split_triple(triple):
    return triple[:, :INNER], triple[:, INNER:2 * INNER], triple[:, 2 * INNER:]


def spread(x, held):
    for t in range(x.shape[1] // 128):
        held[:, t, :] = x[:, t * 128:(t + 1) * 128]


def collect(held, first, count):
    return jnp.concatenate([held[:, t, :] for t in range(first, first + count)], axis=1)


def context_kernel(
    triple, hidden_there, weight, out_t, tokens, packed, held, hidden_in, arrived
):
    fetch = pltpu.make_async_copy(hidden_there, hidden_in, arrived)
    fetch.start()
    w = weight[...].astype(F32)
    o = out_t[...].astype(F32)
    packed[0] = jnp.concatenate(
        [w[:, :PART], o[:, :REST], w[:, PART:], o[:, REST:]], axis=1
    ).astype(BF)
    context = attend_turned(
        triple[:INNER, :], triple[INNER:2 * INNER, :], triple[2 * INNER:, :]
    )
    blank = jnp.zeros((TOKENS, 16 * 128 - D - INNER), F32)
    fetch.wait()
    spread(jnp.concatenate([hidden_in[...].astype(F32), context, blank], axis=1), held)
    tokens[...] = held[...].astype(BF)


def forward_kernel(core, packed, copies, held):
    for i in range(GX):
        held[i * ROWS:(i + 1) * ROWS, :] = packed[i].astype(F32)
    part = jnp.where(core[0] == 0, held[:, :D], held[:, D:]).astype(BF)
    for j in range(GY):
        copies[j] = part


def place_kernel(core, near, tokens, feature_at, placed, near_copy, held):
    held[...] = tokens[...].astype(F32)
    hidden_in = collect(held, 0, 9).astype(BF)
    ctx32 = collect(held, 9, 5)[:, :INNER]
    half = jnp.where(core[0] == 0, ctx32[:, :REST], ctx32[:, REST:]).astype(BF)
    near_copy[...] = near[...]
    mixed = jnp.transpose(nt(near[:, PART:], half))
    placed[...] = nn(hidden_in, pick_columns(D, feature_at[...])) + mixed


def temporal_kernel(
    core, near, far, placed, tokens, cotangent, message, out_rows, held
):
    first = core[0] == 0
    w_near = near[...]
    w_far = far[...]
    near_out = w_near[:, PART:]
    far_out = w_far[:, PART:]
    out_rows[:, :REST] = jnp.where(first, near_out, far_out)
    out_rows[:, REST:] = jnp.where(first, far_out, near_out)
    held[...] = tokens[:, 8:, :].astype(F32)
    ctx32 = collect(held, 1, 5)[:, :INNER]
    half = jnp.where(first, ctx32[:, REST:], ctx32[:, :REST]).astype(BF)

    hidden = (placed[...] + jnp.transpose(nt(far_out, half))).astype(BF).astype(F32)
    centred = hidden - jnp.mean(hidden, axis=-1, keepdims=True)
    scale = lax.rsqrt(jnp.mean(centred * centred, axis=-1, keepdims=True) + 1e-06)
    normal = centred * scale
    normed = normal.astype(BF)
    t_near = nn(normed, w_near)[:, :PART]
    t_far = nn(normed, w_far)[:, :PART]
    triple = jnp.concatenate(
        [jnp.where(first, t_near, t_far), jnp.where(first, t_far, t_near)], axis=1
    ).astype(BF)
    q, k, v = split_triple(triple)
    grads = jnp.concatenate(attend_back(q, k, v, cotangent[...]), axis=1)
    blank = jnp.zeros((TOKENS, REST), F32)
    left = jnp.concatenate([grads[:, :PART], blank], axis=1)
    right = jnp.concatenate([grads[:, PART:], blank], axis=1)
    grad_normal = jnp.transpose(
        nt(w_near, jnp.where(first, left, right).astype(BF))
        + nt(w_far, jnp.where(first, right, left).astype(BF))
    )
    along = jnp.mean(grad_normal * normal, axis=-1, keepdims=True)
    level = jnp.mean(grad_normal, axis=-1, keepdims=True)
    grad_hidden = (scale * (grad_normal - level - normal * along)).astype(BF)
    turned = nn(turn_rows(GX), grad_hidden)
    low, high = turned[:, :INNER], turned[:, INNER:]
    term = tn(grad_hidden, ctx32.astype(BF))
    for j in range(GY):
        message[j] = jnp.concatenate(
            [
                low[j * 8:(j + 1) * 8],
                high[j * 8:(j + 1) * 8],
                term[j * 72:(j + 1) * 72],
            ],
            axis=0,
        ).astype(BF)


def turn_kernel(received, message, held):
    one = received[0].astype(F32)
    total, low, high = one[16:], [one[:8]], [one[8:16]]
    for j in range(1, GY):
        one = received[j].astype(F32)
        total = total + one[16:]
        low.append(one[:8])
        high.append(one[8:16])
    held[:72, :] = total
    held[72:, :] = jnp.zeros((8, INNER), F32)
    turn = turn_rows(GY)
    low = nn(turn, jnp.concatenate(low, axis=0).astype(BF)).astype(BF)
    high = nn(turn, jnp.concatenate(high, axis=0).astype(BF)).astype(BF)
    for i in range(GX):
        message[i, :16, :INNER] = low[i * 16:(i + 1) * 16]
        message[i, :16, INNER:] = high[i * 16:(i + 1) * 16]
        at = i * ROWS
        message[i, 16:, :INNER] = held[at:at + 8, :].astype(BF)
        message[i, 16:, INNER:] = held[at + 8:at + 16, :].astype(BF)


def sum_kernel(received, total):
    s = received[0, 16:, :].astype(F32)
    for i in range(1, GX):
        s = s + received[i, 16:, :].astype(F32)
    total[0, :8] = s[:, :INNER]
    total[0, 8:] = s[:1, INNER:]


def final_kernel(received, out_rows, triple, place_of, grad_triple, grad_hidden):
    grad = received[:, :16, :].reshape(TOKENS, D)
    grad_hidden[...] = nn(grad, pick_columns(D, place_of[...])).astype(BF)
    grads = attend_back_turned(
        triple[:INNER, :],
        triple[INNER:2 * INNER, :],
        triple[2 * INNER:, :],
        nn(grad, out_rows[...]),
    )
    for n, part in enumerate(grads):
        grad_triple[n * INNER:(n + 1) * INNER, :] = part.astype(BF)


def call(kernel, name, outs, *args, scratch=(), there=()):
    many = isinstance(outs, list)
    shapes = [jax.ShapeDtypeStruct(s, t) for s, t in (outs if many else [outs])]
    return pl.pallas_call(
        kernel,
        out_shape=shapes if many else shapes[0],
        in_specs=[
            pl.BlockSpec(
                memory_space=pl.ANY if n in there else pltpu.SMEM if a.ndim == 1 else pltpu.VMEM
            )
            for n, a in enumerate(args)
        ],
        out_specs=(
            [pl.BlockSpec(memory_space=pltpu.VMEM)] * len(shapes)
            if many
            else pl.BlockSpec(memory_space=pltpu.VMEM)
        ),
        scratch_shapes=list(scratch),
        compiler_params=PARAMS,
        name=name,
    )(*args)


def exchange(x, axis):
    return lax.all_to_all(x, axis, 0, 0, tiled=True)


def local(hidden_in, spatial_triple, context_grad, out_weight, triple_weight):
    hidden_in = hidden_in.reshape(TOKENS, D)
    spatial = spatial_triple.reshape(TOKENS, 3 * INNER).T
    cotangent = context_grad.reshape(TOKENS, INNER)

    core = (lax.axis_index("fx") % 2).astype(jnp.int32)[None]
    slabs = (TOKENS, 16, 128)
    held = pltpu.VMEM(slabs, F32)
    tokens, packed = call(
        context_kernel,
        "spatial_context",
        [(slabs, BF), ((1, ROWS, 2 * D), BF)],
        spatial,
        hidden_in,
        triple_weight,
        out_weight.T,
        scratch=[held, pltpu.VMEM((TOKENS, D), BF), pltpu.SemaphoreType.DMA],
        there=(1,),
    )
    tokens = exchange(tokens, ("fx", "fy"))
    packed = lax.all_gather(packed, "fx", axis=0, tiled=True)
    packed, tokens = lax.optimization_barrier((packed, tokens))
    near = call(
        forward_kernel,
        "forward",
        ((GY, 72, D), BF),
        core,
        packed,
        scratch=[pltpu.VMEM((72, 2 * D), F32)],
    )
    near = exchange(near, "fy").reshape(D, D)
    far = lax.ppermute(near, "fx", [(i, i ^ 1) for i in range(GX)])
    placed, near = call(
        place_kernel,
        "hidden_near",
        [((TOKENS, D), F32), ((D, D), BF)],
        core,
        near,
        tokens,
        FEATURE_AT[None],
        scratch=[held],
    )
    message, out_rows = call(
        temporal_kernel,
        "temporal_back",
        [((GY, 88, INNER), BF), ((D, INNER), BF)],
        core,
        near,
        far,
        placed,
        tokens,
        cotangent,
        scratch=[pltpu.VMEM((TOKENS, 8, 128), F32)],
    )
    message = exchange(message, "fy")
    message = call(
        turn_kernel,
        "turn",
        ((GX, 24, D), BF),
        message,
        scratch=[pltpu.VMEM((80, INNER), F32)],
    )
    message = exchange(message, "fx")
    total = call(sum_kernel, "weight_sum", ((1, ROWS, INNER), F32), message)
    totals = lax.all_gather(total, "dp", axis=0, tiled=True)
    grad_triple, grad_hidden = call(
        final_kernel,
        "spatial_back",
        [((3 * INNER, TOKENS), BF), ((TOKENS, D), BF)],
        message,
        out_rows,
        spatial,
        PLACE_OF[None],
    )
    grad_out_weight = (jnp.sum(totals, axis=0) / CLIP_GROUPS).T
    return (
        grad_triple.T.reshape(1, 1, TOKENS, 3 * INNER),
        grad_hidden.reshape(1, 1, TOKENS, D),
        grad_out_weight,
    )


def solution(mesh):
    placed = (
        P("dp", ("fx", "fy"), None, None),
        P("dp", ("fx", "fy"), None, None),
        P("dp", None, ("fx", "fy"), None),
        P(None, ("fx", "fy")),
        P(("fx", "fy"), None),
    )
    return jax.shard_map(
        local,
        mesh=mesh,
        in_specs=placed,
        out_specs=(
            P("dp", ("fx", "fy"), None, None),
            P("dp", ("fx", "fy"), None, None),
            P(None, ("fx", "fy")),
        ),
        check_vma=False,
    )
```
